256 devices in a mesh: stream: 16 (over z, core), cross: 16 (over x, y).
Axes of the slice: x: 4, y: 4, z: 8, core: 2. Of those that a mesh axis runs over, the one named last changes fastest.
Arguments:
- rhs: float32 [1024, 4096], P('stream', 'cross'), may hold values from -6 to 6
- previous: float32 [1024, 4096], P('stream', 'cross'), may hold values from -6 to 6
- dinv: bfloat16 [1024, 64, 4096], P('stream', 'cross'), may hold values from -1 to 2, as said below
- lower: bfloat16 [1024, 64, 4096], P('stream', 'cross'), may hold values from -0.3125 to 0.3125
- spike: bfloat16 [1024, 64, 4096], P('stream', 'cross'), may hold values from -1 to 1.5
- coupling: bfloat16 [1024, 64, 2, 4096], P('stream', 'cross'), may hold values from -0.5 to 0.5
- nbr_line: int32 [1024, 64, 2], P('stream', 'cross'), may hold values from 0 to 63, as said below
- nbr_shift: int32 [1024, 64, 2], P('stream', 'cross'), may hold values from 0 to 2
Outputs:
- sweep: float32 [1024, 4096], P('stream', 'cross')
The draws below stay inside these ranges and needn't reach their ends.
Inputs may be any that keep to these rules, and one draw needn't show every extreme that they name: `dinv`: diagonal entries lie between 0.3 and 1.4, the others are small. `nbr_line`: the lines form a cross-section of rows of 4 lines; every element of line l reaches line l - 4 across one face and line l + 4 across the other, except on the first and last row, where both faces reach the one neighbouring row; which face is which is fixed along each line.
All inputs are finite; a program needn't handle non-finite values.
Results may differ from the reference program's by a relative error of at most 0.0004.
Values sent between devices are 32-bit elements; how exact they have to be, the bound alone decides.
No kernel may reach another device: no remote copies, remote signals or barrier semaphores. Data moves between devices by JAX's collectives and lax.ppermute only.
A program may use at most 128 MiB of HBM per device.

```python
import math
import jax
import jax.numpy as jnp
from jax import lax

UNKNOWNS = 64
SPAN = 16
FACES = 2
L_DEV = 4
ELEMENTS_PER_LINE = 1024
LINE_COUNT = 64


def draw_dinv(key, part):
    key = jax.random.fold_in(key, 11)
    diag_key, jitter_key = jax.random.split(key)
    block_width = UNKNOWNS
    diagonal_block = jax.random.uniform(diag_key, (ELEMENTS_PER_LINE, LINE_COUNT, block_width), jnp.float32, 0.5, 1.2)
    spread = 0.3
    noise = jnp.clip(jax.random.normal(jitter_key, (ELEMENTS_PER_LINE, LINE_COUNT, block_width, block_width), jnp.float32), -4.0, 4.0)
    noise = noise * (spread / math.sqrt(block_width))
    matrix = noise + jnp.eye(block_width, dtype=jnp.float32) * diagonal_block[..., None]
    return matrix.reshape(ELEMENTS_PER_LINE, LINE_COUNT, block_width * block_width).astype(jnp.bfloat16)


def draw_spike(key, part):
    key = jax.random.fold_in(key, 13)
    sluggish_key, decay_key, jump_key, jitter_key = jax.random.split(key, 4)
    block_width = UNKNOWNS
    line_groups = ELEMENTS_PER_LINE // SPAN
    share = 0.5
    slow_mask = jax.random.uniform(sluggish_key, (1, LINE_COUNT, block_width), jnp.float32) < share
    uniform_part = jax.random.uniform(decay_key, (line_groups, LINE_COUNT, block_width), jnp.float32)
    slow_rate = 0.975 + 0.023 * uniform_part
    fast_rate = 0.3 + 0.4 * uniform_part
    decay_rate = jnp.where(slow_mask, slow_rate, fast_rate)
    sudden_jump = jnp.where(jax.random.uniform(jump_key, (line_groups, LINE_COUNT, 1), jnp.float32) < 1.0 / 48.0, 0.75, 1.0)
    exponent = ((jnp.arange(SPAN, dtype=jnp.float32) + 1.0) / SPAN).reshape(1, SPAN, 1, 1)
    diagonal_block = ((decay_rate * sudden_jump)[:, None, :, :] ** exponent).reshape(ELEMENTS_PER_LINE, LINE_COUNT, block_width)
    noise = jnp.clip(jax.random.normal(jitter_key, (ELEMENTS_PER_LINE, LINE_COUNT, block_width, block_width), jnp.float32), -4.0, 4.0)
    noise = noise * (0.15 / math.sqrt(block_width))
    matrix = noise + jnp.eye(block_width, dtype=jnp.float32) * diagonal_block[..., None]
    return matrix.reshape(ELEMENTS_PER_LINE, LINE_COUNT, block_width * block_width).astype(jnp.bfloat16)


def draw_nbr_line(key, part):
    key = jax.random.fold_in(key, 17)
    line_ids = jnp.arange(LINE_COUNT, dtype=jnp.int32)
    below = jnp.where(line_ids < L_DEV, line_ids + L_DEV, line_ids - L_DEV)
    above = jnp.where(line_ids + L_DEV >= LINE_COUNT, line_ids - L_DEV, line_ids + L_DEV)
    flipped = jax.random.randint(key, (LINE_COUNT,), 0, 2, jnp.int32)
    first_face = jnp.where(flipped == 1, above, below)
    second_face = jnp.where(flipped == 1, below, above)
    table = jnp.stack([first_face, second_face], axis=1)
    return jnp.broadcast_to(table[None, :, :], (ELEMENTS_PER_LINE, LINE_COUNT, FACES)).astype(jnp.int32)


def draw_nbr_shift(key, part):
    key = jax.random.fold_in(key, 19)
    raw_value = jax.random.randint(key, (ELEMENTS_PER_LINE, LINE_COUNT, FACES), 0, 4, jnp.int32)
    shifted = jnp.where(raw_value == 0, 0, jnp.where(raw_value == 3, 2, 1))
    return shifted.astype(jnp.int32)


def block_levels(key, shape, cuts, least, high):
    def one(dim, parts):
        steps = jax.random.uniform(jax.random.fold_in(jax.random.fold_in(key, 6), dim), (parts,), jnp.float32, least / len(cuts), high / len(cuts))
        return jnp.repeat(jnp.exp(steps), shape[dim] // parts).reshape((-1,) + (1,) * (len(shape) - dim - 1))

    level = one(*cuts[0])
    for cut in cuts[1:]:
        level = level * one(*cut)
    return level


def bell_draw(key, dims, deviation, limit, cuts=(), held_as=jnp.bfloat16):
    values = jax.random.normal(key, dims, jnp.float32) * deviation
    if len(cuts) > 0:
        values = block_levels(key, dims, cuts, -0.22, 0.18) * values
    return jnp.clip(values, min=-limit, max=limit).astype(held_as)


def setup_inputs(seed: int = 0) -> dict:
    streams_of = jax.random.split(jax.random.key(seed), 9)
    rhs = bell_draw(streams_of[0], (ELEMENTS_PER_LINE, LINE_COUNT * UNKNOWNS), 1.0, 6.0, ((0, 16), (1, 16)), jnp.float32)
    previous = bell_draw(streams_of[1], (ELEMENTS_PER_LINE, LINE_COUNT * UNKNOWNS), 1.0, 6.0, ((0, 16), (1, 16)), jnp.float32)
    dinv = draw_dinv(jax.random.fold_in(streams_of[8], 71), 0)
    lower = bell_draw(streams_of[3], (ELEMENTS_PER_LINE, LINE_COUNT, UNKNOWNS * UNKNOWNS), (6 * UNKNOWNS) ** -0.5, 0.3125, ((0, 16), (1, 16)))
    spike = draw_spike(jax.random.fold_in(streams_of[8], 71), 0)
    coupling = bell_draw(streams_of[5], (ELEMENTS_PER_LINE, LINE_COUNT, FACES, UNKNOWNS * UNKNOWNS), (2 * UNKNOWNS) ** -0.5, 0.5, ((0, 16), (1, 16)))
    nbr_line = draw_nbr_line(jax.random.fold_in(streams_of[8], 71), 0)
    nbr_shift = draw_nbr_shift(jax.random.fold_in(streams_of[8], 71), 0)
    return {"rhs": rhs, "previous": previous, "dinv": dinv, "lower": lower, "spike": spike, "coupling": coupling, "nbr_line": nbr_line, "nbr_shift": nbr_shift}


precise = lax.Precision.HIGHEST


def reference(rhs, previous, dinv, lower, spike, coupling, nbr_line, nbr_shift):
    block_width = UNKNOWNS
    padded = jnp.pad(previous.reshape(ELEMENTS_PER_LINE, LINE_COUNT, block_width), ((1, 1), (0, 0), (0, 0)))
    row_index = jnp.arange(ELEMENTS_PER_LINE, dtype=jnp.int32)[:, None, None] + nbr_shift
    picked = padded[row_index, nbr_line]
    rhs_blocks = rhs.reshape(ELEMENTS_PER_LINE, LINE_COUNT, block_width)
    line_groups = ELEMENTS_PER_LINE // SPAN

    def one_line(line_no):
        def select_line(source):
            return lax.dynamic_index_in_dim(source, line_no, 1, keepdims=False)

        couple_mat = select_line(coupling).astype(jnp.float32).reshape(ELEMENTS_PER_LINE, FACES, block_width, block_width)
        nearby = select_line(picked)
        residual = select_line(rhs_blocks) - jnp.einsum("efij,efj->ei", couple_mat, nearby, precision=precise)
        residual = residual.reshape(line_groups, SPAN, block_width)
        inverse_mat = select_line(dinv).astype(jnp.float32).reshape(line_groups, SPAN, block_width, block_width)
        lower_mat = select_line(lower).astype(jnp.float32).reshape(line_groups, SPAN, block_width, block_width)
        spike_mat = select_line(spike).astype(jnp.float32).reshape(line_groups, SPAN, block_width, block_width)
        earlier = jnp.zeros((line_groups, block_width), jnp.float32)
        collected = []
        for position in range(SPAN):
            balance = residual[:, position] - jnp.einsum("bij,bj->bi", lower_mat[:, position], earlier, precision=precise)
            earlier = jnp.einsum("bij,bj->bi", inverse_mat[:, position], balance, precision=precise)
            collected.append(earlier)
        local_sol = jnp.stack(collected, axis=1)

        def advance(inflow, inputs):
            spike_last, local_last = inputs
            return local_last + jnp.dot(spike_last, inflow, precision=precise), inflow

        start_flow = jnp.zeros((block_width,), jnp.float32)
        _, inflows = lax.scan(advance, start_flow, (spike_mat[:, SPAN - 1], local_sol[:, SPAN - 1]))
        result = local_sol + jnp.einsum("bkij,bj->bki", spike_mat, inflows, precision=precise)
        return result.reshape(ELEMENTS_PER_LINE, block_width)

    swept = lax.map(one_line, jnp.arange(LINE_COUNT, dtype=jnp.int32))
    return jnp.transpose(swept, (1, 0, 2)).reshape(ELEMENTS_PER_LINE, LINE_COUNT * block_width)
```

```python
import functools

import jax
import jax.numpy as jnp
from jax import lax
from jax.experimental import pallas as pl
from jax.experimental.pallas import tpu as pltpu
from jax.sharding import PartitionSpec as P

WIDTH = 64
SPAN = 16
LANES = 128
F32 = jnp.float32
BF16 = jnp.bfloat16


def iota(shape, dim):
    return lax.broadcasted_iota(jnp.int32, shape, dim)


def swap_halves(x):
    return jnp.concatenate([x[:, WIDTH:], x[:, :WIDTH]], axis=1)


def dot(a, b):
    return jnp.dot(a, b, preferred_element_type=F32)


def dot_t(a, b):
    return lax.dot_general(a, b, (((1,), (1,)), ((), ())), preferred_element_type=F32)


def split(x):
    high = x.astype(BF16)
    return high, (x - high.astype(F32)).astype(BF16)


def both(x):
    high = x.astype(BF16).astype(F32)
    return jnp.concatenate([high, x - high], axis=0).astype(BF16)


def fold(y):
    return y[:8] + y[8:]


def order_rows():
    row, col = iota((256, 256), 0), iota((256, 256), 1)
    line, i = row // WIDTH, row % WIDTH
    swapped = (i % 2) != (line % 2)
    want = 4 * (i // 2) + line + jnp.where(swapped, LANES, 0)
    return jnp.where(col == want, 1.0, 0.0).astype(BF16)


def half_mask(rows):
    return (iota((rows, LANES), 0) // WIDTH) % 2 == iota((rows, LANES), 1) // WIDTH


def paired(x, order):
    both_ways = jnp.concatenate([x, swap_halves(x)], axis=0)
    y = dot(order, both_ways)
    return jnp.where(half_mask(256), y, 0.0).astype(BF16)


def expand(c):
    s = swap_halves(c)
    low = iota(c.shape, 1) < WIDTH
    mask = half_mask(LANES)
    return (
        jnp.where(mask, jnp.where(low, c, s), 0.0),
        jnp.where(mask, jnp.where(low, s, c), 0.0),
    )


def device_map_kernel(spike_ref, out_ref, order_ref):
    b = pl.program_id(0)

    @pl.when(b == 0)
    def _():
        order_ref[...] = order_rows()

    m = paired(spike_ref[0], order_ref[...])
    low = iota((LANES, LANES), 1) < WIDTH

    @pl.when(b == 0)
    def _():
        m0, m1 = m[:LANES].astype(F32), m[LANES:].astype(F32)
        out_ref[...] = jnp.where(low, m0 + swap_halves(m0), m1 + swap_halves(m1))

    @pl.when(b > 0)
    def _():
        high, rest = split(out_ref[...])
        y = dot(m, high) + dot(m, rest)
        out_ref[...] = jnp.where(low, y[:LANES], y[LANES:])


def device_map(spike):
    blocks = spike.shape[0] // SPAN
    return pl.pallas_call(
        device_map_kernel,
        grid=(blocks,),
        in_specs=[pl.BlockSpec((1, LANES, LANES), lambda b: (SPAN * b + SPAN - 1, 0, 0))],
        out_specs=pl.BlockSpec((LANES, LANES), lambda b: (0, 0)),
        out_shape=jax.ShapeDtypeStruct((LANES, LANES), F32),
        scratch_shapes=[pltpu.VMEM((256, 256), BF16)],
        name="device_map",
    )(spike)


def product_kernel(upper_ref, own_ref, other_ref, out_ref):
    upper = upper_ref[0] > 0
    own, other = own_ref[...], other_ref[...]
    after = jnp.where(upper, own, other)
    before_h, before_l = split(jnp.where(upper, other, own))
    low = iota((LANES, LANES), 1) < WIDTH
    parts = []
    for m in expand(after):
        high, rest = split(m)
        parts.append(dot(high, before_h) + dot(rest, before_h) + dot(high, before_l))
    out_ref[...] = jnp.where(low, parts[0], parts[1])


def product(upper, own, other):
    return pl.pallas_call(
        product_kernel,
        in_specs=[
            pl.BlockSpec(memory_space=pltpu.SMEM),
            pl.BlockSpec(memory_space=pltpu.VMEM),
            pl.BlockSpec(memory_space=pltpu.VMEM),
        ],
        out_specs=pl.BlockSpec(memory_space=pltpu.VMEM),
        out_shape=jax.ShapeDtypeStruct((LANES, LANES), F32),
        name="product",
    )(upper, own, other)


def arrange_kernel(*refs):
    count = (len(refs) - 1) // 2
    order_ref = refs[-1]

    @pl.when(pl.program_id(0) == 0)
    def _():
        order_ref[...] = order_rows()

    order = order_ref[...]
    for src, dst in zip(refs[:count], refs[count : 2 * count]):
        for e in range(src.shape[0]):
            dst[e] = paired(src[e], order)


def arrange(*arrays):
    n = arrays[0].shape[0]
    step = 8
    return pl.pallas_call(
        arrange_kernel,
        grid=(n // step,),
        in_specs=[pl.BlockSpec((step, LANES, LANES), lambda e: (e, 0, 0))] * len(arrays),
        out_specs=[pl.BlockSpec((step, 256, LANES), lambda e: (e, 0, 0))] * len(arrays),
        out_shape=[jax.ShapeDtypeStruct((n, 256, LANES), BF16)] * len(arrays),
        scratch_shapes=[pltpu.VMEM((256, 256), BF16)],
        cost_estimate=pl.CostEstimate(
            flops=2 * len(arrays) * n * 256 * 256 * 128,
            bytes_accessed=len(arrays) * n * 3 * 32768,
            transcendentals=0,
        ),
        name="arrange",
    )(*arrays)


def times_blocks(x, mats):
    lhs = both(x)
    row = iota((8, LANES), 0)
    y = None
    for b, m in enumerate(mats):
        part = fold(dot_t(lhs, m))
        y = part if y is None else jnp.where(row == b, part, y)
    return y


def times_map(x, c_parts):
    lhs = both(x)
    high, rest = c_parts
    y = dot_t(lhs, high)
    return fold(y) + dot_t(lhs, rest)[:8]


def local_kernel(
    me_ref,
    code_ref,
    low_ref,
    high_ref,
    rhs_ref,
    coupling_hbm,
    lower_hbm,
    dinv_hbm,
    spike_hbm,
    t1_ref,
    t2_ref,
    t4_ref,
    g_ref,
    send_ref,
    coupling_v,
    lower_v,
    dinv_v,
    spike_v,
    vec,
    raw,
    res,
    sol,
    sems,
):
    n = rhs_ref.shape[0]
    blocks = n // SPAN
    copies = [
        pltpu.make_async_copy(coupling_hbm, coupling_v, sems.at[0]),
        pltpu.make_async_copy(lower_hbm, lower_v, sems.at[1]),
        pltpu.make_async_copy(dinv_hbm, dinv_v, sems.at[2]),
    ]
    for b in range(1, blocks):
        copies.append(
            pltpu.make_async_copy(spike_hbm.at[SPAN * b + SPAN - 1], spike_v.at[b], sems.at[2 + b])
        )
    for c in copies:
        c.start()

    code = code_ref[...].astype(BF16)
    r8, c8 = iota((8, 512), 0), iota((8, 512), 1)
    spread = jnp.where((r8 // 2 == (c8 % 256) // WIDTH) & (r8 % 2 == c8 // 256), 1.0, 0.0)
    where = lax.dot_general(
        code, spread.astype(BF16), (((0,), (0,)), ((), ())), preferred_element_type=F32
    )
    sides = (low_ref, high_ref)
    lane = iota((n, LANES), 1)
    for f in range(2):
        for p in range(2):
            lanes = slice(LANES * p, LANES * (p + 1))
            w = where[:, 256 * f + LANES * p : 256 * f + LANES * (p + 1)]
            x = jnp.zeros((n, LANES), F32)
            for side in range(2):
                for s in range(3):
                    x = jnp.where(w == float(3 * side + s), sides[side][pl.ds(s, n), lanes], x)
            top = x.astype(BF16).astype(F32)
            for h, part in enumerate((top, x - top)):
                turned = swap_halves(part)
                for q in range(2):
                    for a in range(2):
                        v = jnp.where(lane // WIDTH == a, part if a == q else turned, 0.0)
                        vec[2 * p + h, pl.ds(4 * q + 2 * f + a, n, stride=8), :] = v

    copies[0].wait()
    for e in range(n):
        for p in range(2):
            lhs = jnp.concatenate(
                [vec[2 * p, 8 * e : 8 * e + 8, :], vec[2 * p + 1, 8 * e : 8 * e + 8, :]], axis=0
            ).astype(BF16)
            raw[p, 8 * e : 8 * e + 8, :] = fold(
                dot_t(lhs, coupling_v[e, LANES * p : LANES * (p + 1), :])
            )
    even = lane % 2 == 0
    for p in range(2):
        y = None
        for a in range(2):
            acc = jnp.zeros((n, LANES), F32)
            for q in range(2):
                for f in range(2):
                    z = raw[p, pl.ds(4 * q + 2 * f + a, n, stride=8), :]
                    acc = jnp.where((lane // WIDTH == q) & (lane % 2 == f), z, acc)
            acc = acc + jnp.where(even, pltpu.roll(acc, LANES - 1, 1), pltpu.roll(acc, 1, 1))
            y = acc if a == 0 else jnp.where(even, y, acc)
        residual = rhs_ref[:, LANES * p : LANES * (p + 1)] - y
        for b in range(blocks):
            res[p, pl.ds(b, SPAN, stride=8), :] = residual[SPAN * b : SPAN * (b + 1)]

    for c in copies[1:]:
        c.wait()
    g = [None, None]
    for k in range(SPAN):
        for p in range(2):
            rows = slice(LANES * p, LANES * (p + 1))
            balance = res[p, 8 * k : 8 * k + 8, :]
            if k > 0:
                balance = balance - times_blocks(
                    g[p], [lower_v[SPAN * b + k, rows, :] for b in range(blocks)]
                )
            g[p] = times_blocks(balance, [dinv_v[SPAN * b + k, rows, :] for b in range(blocks)])
            sol[p, 8 * k : 8 * k + 8, :] = g[p]
    me = me_ref[0]
    for p in range(2):
        lanes = slice(LANES * p, LANES * (p + 1))
        for b in range(blocks):
            g_ref[SPAN * b : SPAN * (b + 1), lanes] = sol[p, pl.ds(b, SPAN, stride=8), :]
        last = sol[p, 8 * (SPAN - 1) : 8 * SPAN, :]
        out = last[0:1]
        for b in range(1, blocks):
            x = jnp.broadcast_to(out, (8, LANES))
            out = fold(dot_t(both(x), spike_v[b, lanes, :]))[0:1] + last[b : b + 1]
        w = jnp.broadcast_to(out, (8, LANES))
        levels = [w]
        for m, t_ref in ((1, t1_ref), (2, t2_ref), (4, t4_ref)):
            moved = times_map(w, split(expand(t_ref[...])[p]))
            w = jnp.where((me // m) % 2 == 0, moved, w)
            levels.append(w)
        for half in range(2):
            target = iota((8, LANES), 0) + 8 * half
            message = jnp.zeros((8, LANES), F32)
            for lev, m in enumerate((1, 2, 4, 8)):
                reach = (target // (2 * m) == me // (2 * m)) & (target // m == me // m + 1)
                message = jnp.where(reach, levels[lev], message)
            send_ref[8 * half : 8 * half + 8, lanes] = message


def local(me, code, low, high, rhs, coupling, lower, dinv, spike, t1, t2, t4):
    n = rhs.shape[0]
    blocks = n // SPAN
    vmem = pl.BlockSpec(memory_space=pltpu.VMEM)
    hbm = pl.BlockSpec(memory_space=pl.ANY)
    return pl.pallas_call(
        local_kernel,
        in_specs=[pl.BlockSpec(memory_space=pltpu.SMEM)] + [vmem] * 4 + [hbm] * 4 + [vmem] * 3,
        out_specs=[vmem, vmem],
        out_shape=[
            jax.ShapeDtypeStruct((n, 256), F32),
            jax.ShapeDtypeStruct((16, 256), F32),
        ],
        scratch_shapes=[
            pltpu.VMEM((n, 256, LANES), BF16),
            pltpu.VMEM((n, 256, LANES), BF16),
            pltpu.VMEM((n, 256, LANES), BF16),
            pltpu.VMEM((blocks, 256, LANES), BF16),
            pltpu.VMEM((4, 8 * n, LANES), F32),
            pltpu.VMEM((2, 8 * n, LANES), F32),
            pltpu.VMEM((2, 8 * SPAN, LANES), F32),
            pltpu.VMEM((2, 8 * SPAN, LANES), F32),
            pltpu.SemaphoreType.DMA((2 + blocks,)),
        ],
        compiler_params=pltpu.CompilerParams(vmem_limit_bytes=40 << 20),
        name="local",
    )(me, code, low, high, rhs, coupling, lower, dinv, spike, t1, t2, t4)


def finish_kernel(me_ref, got_ref, g_ref, t1_ref, t2_ref, t4_ref, spike_hbm, out_ref, spike_v, sem):
    n = g_ref.shape[0]
    blocks = n // SPAN
    copy = pltpu.make_async_copy(spike_hbm, spike_v, sem)
    copy.start()
    me = me_ref[0]
    source = iota((16, LANES), 0)
    flows = []
    for p in range(2):
        lanes = slice(LANES * p, LANES * (p + 1))
        got = got_ref[:, lanes]
        v = None
        for m, t_ref in ((8, None), (4, t4_ref), (2, t2_ref), (1, t1_ref)):
            from_here = (source // (2 * m) == me // (2 * m)) & (source // m + 1 == me // m)
            part = jnp.sum(jnp.where(from_here, got, 0.0), axis=0, keepdims=True)
            part = jnp.broadcast_to(part, (8, LANES))
            if v is None:
                v = part
            else:
                moved = times_map(v, split(expand(t_ref[...])[p]))
                v = jnp.where((me // m) % 2 == 1, moved, v) + part
        flows.append([v])
    copy.wait()
    for b in range(blocks):
        for p in range(2):
            lanes = slice(LANES * p, LANES * (p + 1))
            x = flows[p][b]
            lhs = both(x)
            for k in range(SPAN - 1, -1, -1):
                e = SPAN * b + k
                y = fold(dot_t(lhs, spike_v[e, lanes, :]))[0:1] + g_ref[e : e + 1, lanes]
                out_ref[e : e + 1, lanes] = y
                if k == SPAN - 1:
                    flows[p].append(jnp.broadcast_to(y, (8, LANES)))


def finish(me, got, g, t1, t2, t4, spike):
    n = g.shape[0]
    vmem = pl.BlockSpec(memory_space=pltpu.VMEM)
    return pl.pallas_call(
        finish_kernel,
        in_specs=[pl.BlockSpec(memory_space=pltpu.SMEM)]
        + [vmem] * 5
        + [pl.BlockSpec(memory_space=pl.ANY)],
        out_specs=vmem,
        out_shape=jax.ShapeDtypeStruct((n, 256), F32),
        scratch_shapes=[pltpu.VMEM((n, 256, LANES), BF16), pltpu.SemaphoreType.DMA],
        compiler_params=pltpu.CompilerParams(vmem_limit_bytes=32 << 20),
        name="finish",
    )(me, got, g, t1, t2, t4, spike)


def flip(x, axis, bit):
    count = lax.axis_size(axis)
    return lax.ppermute(x, axis, [(i, i ^ bit) for i in range(count)])


def between(x, axis):
    count = lax.axis_size(axis)
    pairs = [(i, i + 1) for i in range(1, count - 1, 2)]
    return lax.ppermute(x, axis, pairs + [(j, i) for i, j in pairs])


def on_device(rhs, previous, dinv, lower, spike, coupling, nbr_line, nbr_shift):
    n = rhs.shape[0]
    stream, cross = lax.axis_index("stream"), lax.axis_index("cross")
    me = stream.reshape(1)

    def as_it_lies(x):
        return x.reshape(n, 4, 32, LANES).transpose(0, 2, 1, 3).reshape(n, LANES, LANES)

    even = stream % 2 == 0
    first, last = previous[:1], previous[n - 1 :]
    mate = flip(jnp.where(even, last, first), "stream", 1)
    beyond = between(jnp.where(even, first, last), "stream")
    bordered = jnp.concatenate(
        [jnp.where(even, beyond, mate), previous, jnp.where(even, mate, beyond)], axis=0
    )
    far = between(bordered, "cross")
    near = flip(bordered, "cross", 1)
    low = jnp.where(cross % 2 == 0, far, near)
    high = jnp.where(cross % 2 == 0, near, far)

    line = cross * 4 + lax.broadcasted_iota(jnp.int32, nbr_line.shape, 1)
    code = (jnp.where(nbr_line > line, 3, 0) + nbr_shift).astype(F32)
    code = code.transpose(1, 2, 0).reshape(8, n)

    spike_x = as_it_lies(spike)
    own1 = device_map(spike_x)
    t1 = flip(own1, "stream", 1)
    own2 = product(me % 2, own1, t1)
    t2 = flip(own2, "stream", 2)
    own4 = product((me // 2) % 2, own2, t2)
    t4 = flip(own4, "stream", 4)
    lower_m, dinv_m, spike_m = arrange(as_it_lies(lower), as_it_lies(dinv), spike_x)
    coupling_x = (
        coupling.reshape(n, 4, 2, 32, LANES).transpose(0, 1, 3, 2, 4).reshape(n, 256, LANES)
    )
    g, send = local(me, code, low, high, rhs, coupling_x, lower_m, dinv_m, spike_m, t1, t2, t4)
    got = lax.all_to_all(send, "stream", 0, 0, tiled=True)
    return finish(me, got, g, t1, t2, t4, spike_m)


def solution(mesh):
    return jax.shard_map(
        on_device,
        mesh=mesh,
        in_specs=(
            P("stream", "cross"),
            P("stream", "cross"),
            P("stream", "cross", None),
            P("stream", "cross", None),
            P("stream", "cross", None),
            P("stream", "cross", None, None),
            P("stream", "cross", None),
            P("stream", "cross", None),
        ),
        out_specs=P("stream", "cross"),
        check_vma=False,
    )
```

```python
import functools

import jax
import jax.numpy as jnp
from jax import lax
from jax.experimental import pallas as pl
from jax.experimental.pallas import tpu as pltpu
from jax.sharding import PartitionSpec as P

WIDTH = 64
SPAN = 16
LANES = 128
F32 = jnp.float32
BF16 = jnp.bfloat16


def iota(shape, dim):
    return lax.broadcasted_iota(jnp.int32, shape, dim)


def swap_halves(x):
    return jnp.concatenate([x[:, WIDTH:], x[:, :WIDTH]], axis=1)


def dot(a, b):
    return jnp.dot(a, b, preferred_element_type=F32)


def dot_t(a, b):
    return lax.dot_general(a, b, (((1,), (1,)), ((), ())), preferred_element_type=F32)


def split(x):
    high = x.astype(BF16)
    return high, (x - high.astype(F32)).astype(BF16)


def both(x):
    high = x.astype(BF16).astype(F32)
    return jnp.concatenate([high, x - high], axis=0).astype(BF16)


def fold(y):
    return y[:8] + y[8:]


def order_rows():
    row, col = iota((256, 256), 0), iota((256, 256), 1)
    line, i = row // WIDTH, row % WIDTH
    swapped = (i % 2) != (line % 2)
    want = 4 * (i // 2) + line + jnp.where(swapped, LANES, 0)
    return jnp.where(col == want, 1.0, 0.0).astype(BF16)


def half_mask(rows):
    return (iota((rows, LANES), 0) // WIDTH) % 2 == iota((rows, LANES), 1) // WIDTH


def paired(x, order):
    both_ways = jnp.concatenate([x, swap_halves(x)], axis=0)
    y = dot(order, both_ways)
    return jnp.where(half_mask(256), y, 0.0).astype(BF16)


def expand(c):
    s = swap_halves(c)
    low = iota(c.shape, 1) < WIDTH
    mask = half_mask(LANES)
    return (
        jnp.where(mask, jnp.where(low, c, s), 0.0),
        jnp.where(mask, jnp.where(low, s, c), 0.0),
    )


def device_map_kernel(spike_hbm, out_ref, spike_v, sems):
    blocks = spike_v.shape[0]
    copies = [
        pltpu.make_async_copy(spike_hbm.at[SPAN * b + SPAN - 1], spike_v.at[b], sems.at[b])
        for b in range(blocks)
    ]
    for c in copies:
        c.start()
    order = order_rows()
    low = iota((LANES, LANES), 1) < WIDTH
    for b in range(blocks):
        copies[b].wait()
        m = paired(spike_v[b], order)
        if b == 0:
            m0, m1 = m[:LANES].astype(F32), m[LANES:].astype(F32)
            c = jnp.where(low, m0 + swap_halves(m0), m1 + swap_halves(m1))
        else:
            high, rest = split(c)
            y = dot(m, high) + dot(m, rest)
            c = jnp.where(low, y[:LANES], y[LANES:])
    out_ref[...] = c


ALMOST_ALL = 53 << 20
MOST = 49 << 20
VMEM = pl.BlockSpec(memory_space=pltpu.VMEM)
SMEM = pl.BlockSpec(memory_space=pltpu.SMEM)
HBM = pl.BlockSpec(memory_space=pltpu.HBM)


def device_map(spike):
    blocks = spike.shape[0] // SPAN
    return pl.pallas_call(
        device_map_kernel,
        in_specs=[HBM],
        out_specs=VMEM,
        out_shape=jax.ShapeDtypeStruct((LANES, LANES), F32),
        scratch_shapes=[
            pltpu.VMEM((blocks, LANES, LANES), BF16),
            pltpu.SemaphoreType.DMA((blocks,)),
        ],
        compiler_params=pltpu.CompilerParams(vmem_limit_bytes=ALMOST_ALL),
        name="device_map",
    )(spike)


def product_kernel(upper_ref, own_ref, other_ref, out_ref):
    upper = upper_ref[0] > 0
    own, other = own_ref[...], other_ref[...]
    after = jnp.where(upper, own, other)
    before_h, before_l = split(jnp.where(upper, other, own))
    low = iota((LANES, LANES), 1) < WIDTH
    parts = []
    for m in expand(after):
        high, rest = split(m)
        parts.append(dot(high, before_h) + dot(rest, before_h) + dot(high, before_l))
    out_ref[...] = jnp.where(low, parts[0], parts[1])


def product(upper, own, other):
    return pl.pallas_call(
        product_kernel,
        in_specs=[
            pl.BlockSpec(memory_space=pltpu.SMEM),
            pl.BlockSpec(memory_space=pltpu.VMEM),
            pl.BlockSpec(memory_space=pltpu.VMEM),
        ],
        out_specs=pl.BlockSpec(memory_space=pltpu.VMEM),
        out_shape=jax.ShapeDtypeStruct((LANES, LANES), F32),
        compiler_params=pltpu.CompilerParams(vmem_limit_bytes=4 << 20),
        name="product",
    )(upper, own, other)


def times_map(x, c_parts):
    lhs = both(x)
    high, rest = c_parts
    return fold(dot_t(lhs, high)) + dot_t(lhs, rest)[:8]


def reduce_lanes():
    row, col = iota((256, LANES), 0), iota((256, LANES), 1)
    return jnp.where(col % 2 == (row % LANES) // WIDTH, 1.0, 0.0).astype(BF16)


def own_lane():
    return iota((LANES, LANES), 0) // 4 == (iota((LANES, LANES), 1) % WIDTH) // 2


def lying_matvec(x, m, sums, own):
    prod = (m.astype(F32).reshape(16, 8, LANES) * x[None]).reshape(LANES, LANES)
    high = prod.astype(BF16)
    rest = (prod - high.astype(F32)).astype(BF16)
    z = dot(jnp.concatenate([high, rest], axis=1), sums)
    z = jnp.sum(jnp.where(own, z, 0.0).reshape(16, 8, LANES), axis=0)
    return z + pltpu.roll(z, 4, 0)


def line_rows(natural, p, q):
    lane = iota(natural.shape, 1)
    return jnp.where(lane // WIDTH == q, natural, swap_halves(natural))


def look_up(code_ref):
    code = code_ref[...].astype(BF16)
    r8, c8 = iota((8, 512), 0), iota((8, 512), 1)
    spread = jnp.where((r8 // 2 == (c8 % 256) // WIDTH) & (r8 % 2 == c8 // 256), 1.0, 0.0)
    return lax.dot_general(
        code, spread.astype(BF16), (((0,), (0,)), ((), ())), preferred_element_type=F32
    )


def residual_rows(n, where, rows_at, rhs, blocks_of, vec, raw):
    lane = iota((n, LANES), 1)
    for f in range(2):
        for p in range(2):
            w = where[:, 256 * f + LANES * p : 256 * f + LANES * (p + 1)]
            x = jnp.zeros((n, LANES), F32)
            for side in range(2):
                for s in range(3):
                    x = jnp.where(w == float(3 * side + s), rows_at(side, s, p), x)
            top = x.astype(BF16).astype(F32)
            for h, part in enumerate((top, x - top)):
                turned = swap_halves(part)
                for q in range(2):
                    for a in range(2):
                        v = jnp.where(lane // WIDTH == a, part if a == q else turned, 0.0)
                        vec[2 * p + h, pl.ds(4 * q + 2 * f + a, n, stride=8), :] = v

    for t, blocks in blocks_of:
        for p in range(2):
            lhs = jnp.concatenate(
                [vec[2 * p, 8 * t : 8 * t + 8, :], vec[2 * p + 1, 8 * t : 8 * t + 8, :]], axis=0
            ).astype(BF16)
            raw[p, 8 * t : 8 * t + 8, :] = fold(dot_t(lhs, blocks(p)))
    even = lane % 2 == 0
    lines = []
    for p in range(2):
        y = None
        for a in range(2):
            acc = jnp.zeros((n, LANES), F32)
            for q in range(2):
                for f in range(2):
                    z = raw[p, pl.ds(4 * q + 2 * f + a, n, stride=8), :]
                    acc = jnp.where((lane // WIDTH == q) & (lane % 2 == f), z, acc)
            acc = acc + jnp.where(even, pltpu.roll(acc, LANES - 1, 1), pltpu.roll(acc, 1, 1))
            y = acc if a == 0 else jnp.where(even, y, acc)
        residual = rhs[:, LANES * p : LANES * (p + 1)] - y
        for q in range(2):
            lines.append((2 * p + q, line_rows(residual, p, q)))
    return lines


def residual_kernel(code_ref, low_ref, high_ref, rhs_ref, coupling_hbm, lower_hbm, dinv_hbm, *rest):
    res, ends_ref, ends_coupling, lower_v, dinv_v, coupling_v, sides, vec, raw, sems = rest
    n = rhs_ref.shape[0]
    cuts = [0, n // 8, n // 4, n // 2, n]
    copies = {
        lo: pltpu.make_async_copy(
            coupling_hbm.at[pl.ds(lo, hi - lo)], coupling_v.at[pl.ds(lo, hi - lo)], sems.at[i]
        )
        for i, (lo, hi) in enumerate(zip(cuts, cuts[1:]))
    }
    later = [
        pltpu.make_async_copy(lower_hbm, lower_v, sems.at[4]),
        pltpu.make_async_copy(dinv_hbm, dinv_v, sems.at[5]),
    ]
    for c in list(copies.values()) + later:
        c.start()
    where = look_up(code_ref)
    ends_ref[0:1, :] = where[0:1]
    ends_ref[1:2, :] = where[n - 1 : n]
    for side, ref in enumerate((low_ref, high_ref)):
        sides[side, 0:8, :] = jnp.zeros((8, 256), F32)
        sides[side, 8 : n + 8, :] = ref[...]
        sides[side, n + 8 : n + 16, :] = jnp.zeros((8, 256), F32)

    def rows_at(side, s, p):
        return sides[side, pl.ds(7 + s, n), LANES * p : LANES * (p + 1)]

    def blocks_of():
        for e in range(n):
            if e in copies:
                copies[e].wait()
            yield e, lambda p: coupling_v[e, LANES * p : LANES * (p + 1), :]

    for line, rows in residual_rows(n, where, rows_at, rhs_ref[...], blocks_of(), vec, raw):
        res[pl.ds(line, n, stride=8), :] = rows
        res[pl.ds(line + 4, n, stride=8), :] = rows
    ends_coupling[0] = coupling_v[0]
    ends_coupling[1] = coupling_v[n - 1]
    for c in later:
        c.wait()


def residual(code, low, high, rhs, coupling, lower, dinv):
    n = rhs.shape[0]
    return pl.pallas_call(
        residual_kernel,
        in_specs=[VMEM] * 4 + [HBM] * 3,
        out_specs=[VMEM] * 5,
        out_shape=[
            jax.ShapeDtypeStruct((8 * n, LANES), F32),
            jax.ShapeDtypeStruct((2, 512), F32),
            jax.ShapeDtypeStruct((2, 256, LANES), BF16),
            jax.ShapeDtypeStruct(lower.shape, BF16),
            jax.ShapeDtypeStruct(dinv.shape, BF16),
        ],
        scratch_shapes=[
            pltpu.VMEM((n, 256, LANES), BF16),
            pltpu.VMEM((2, n + 16, 256), F32),
            pltpu.VMEM((4, 8 * n, LANES), F32),
            pltpu.VMEM((2, 8 * n, LANES), F32),
            pltpu.SemaphoreType.DMA((6,)),
        ],
        compiler_params=pltpu.CompilerParams(vmem_limit_bytes=MOST),
        cost_estimate=pl.CostEstimate(flops=10**8, bytes_accessed=4 << 20, transcendentals=0),
        name="residual",
    )(code, low, high, rhs, coupling, lower, dinv)


def edge_terms(t, code, edge, blocks):
    row, lane = iota((8, LANES), 0), iota((8, LANES), 1)
    q, f, a = row // 4, (row // 2) % 2, row % 2
    lines = jnp.zeros((8, LANES), F32)
    for p in range(2):
        lanes = slice(LANES * p, LANES * (p + 1))
        below = jnp.broadcast_to(edge[2 * t : 2 * t + 1, lanes], (8, LANES))
        above = jnp.broadcast_to(edge[2 * t + 1 : 2 * t + 2, lanes], (8, LANES))
        w = jnp.where(f == 0, code[t : t + 1, lanes], code[t : t + 1, 256 + LANES * p : 256 + LANES * (p + 1)])
        x = jnp.where(w == 2.0 * t, below, jnp.where(w == 3.0 + 2.0 * t, above, 0.0))
        x = jnp.where(lane // WIDTH == a, jnp.where(a == q, x, swap_halves(x)), 0.0)
        y = fold(dot_t(both(x), blocks(p)))
        y = jnp.where((lane // WIDTH == q) & (lane % 2 == f), y, 0.0)
        y = y + jnp.where(lane % 2 == 0, pltpu.roll(y, LANES - 1, 1), pltpu.roll(y, 1, 1))
        y = jnp.sum(jnp.where(lane % 2 == a, y, 0.0), axis=0, keepdims=True)
        y = jnp.broadcast_to(y, (8, LANES))
        for h in range(2):
            lines = jnp.where(row % 4 == 2 * p + h, line_rows(y, p, h), lines)
    return lines


def chain_kernel(
    res, ends_ref, edge_ref, coupling_ref, lower_ref, dinv_ref, spike_hbm, g_ref, out_ref, sol, spike_v, sems
):
    n = g_ref.shape[0]
    blocks = n // SPAN
    ends = (0, n - 1)
    spike_copies = [
        pltpu.make_async_copy(spike_hbm.at[SPAN * b + SPAN - 1], spike_v.at[b], sems.at[b])
        for b in range(1, blocks)
    ]
    for c in spike_copies:
        c.start()
    code, edge = ends_ref[...], edge_ref[...]
    terms = [
        edge_terms(t, code, edge, lambda p, t=t: coupling_ref[t, LANES * p : LANES * (p + 1), :])
        for t in range(2)
    ]
    sums, own = reduce_lanes(), own_lane()
    g = [None] * blocks
    for k in range(SPAN):
        for b in range(blocks):
            e = SPAN * b + k
            balance = res[8 * e : 8 * e + 8, :]
            if e in ends:
                balance = balance - terms[ends.index(e)]
            if k > 0:
                balance = balance - lying_matvec(g[b], lower_ref[e], sums, own)
            g[b] = lying_matvec(balance, dinv_ref[e], sums, own)
            sol[8 * e : 8 * e + 8, :] = g[b]
    for c in spike_copies:
        c.wait()
    out = g[0]
    for b in range(1, blocks):
        out = lying_matvec(out, spike_v[b], sums, own) + g[b]
    out_ref[...] = out
    lane = iota((n, LANES), 1)
    for p in range(2):
        g_ref[:, LANES * p : LANES * (p + 1)] = jnp.where(
            lane < WIDTH, sol[pl.ds(2 * p, n, stride=8), :], sol[pl.ds(2 * p + 1, n, stride=8), :]
        )


def chain(res, ends, edge, coupling, lower, dinv, spike):
    n = lower.shape[0]
    blocks = n // SPAN
    return pl.pallas_call(
        chain_kernel,
        in_specs=[VMEM] * 6 + [HBM],
        out_specs=[VMEM, VMEM],
        out_shape=[
            jax.ShapeDtypeStruct((n, 256), F32),
            jax.ShapeDtypeStruct((8, LANES), F32),
        ],
        scratch_shapes=[
            pltpu.VMEM((8 * n, LANES), F32),
            pltpu.VMEM((blocks, LANES, LANES), BF16),
            pltpu.SemaphoreType.DMA((blocks,)),
        ],
        compiler_params=pltpu.CompilerParams(vmem_limit_bytes=MOST),
        cost_estimate=pl.CostEstimate(flops=10**9, bytes_accessed=4 << 20, transcendentals=0),
        name="chain",
    )(res, ends, edge, coupling, lower, dinv, spike)


def outflow_kernel(me_ref, out_ref, t1_ref, t2_ref, t4_ref, send_ref):
    me = me_ref[0]
    out = out_ref[...]
    for p in range(2):
        lanes = slice(LANES * p, LANES * (p + 1))
        w = jnp.where(iota((1, LANES), 1) < WIDTH, out[2 * p : 2 * p + 1], out[2 * p + 1 : 2 * p + 2])
        w = jnp.broadcast_to(w, (8, LANES))
        levels = [w]
        for m, t_ref in ((1, t1_ref), (2, t2_ref), (4, t4_ref)):
            moved = times_map(w, split(expand(t_ref[...])[p]))
            w = jnp.where((me // m) % 2 == 0, moved, w)
            levels.append(w)
        for half in range(2):
            target = iota((8, LANES), 0) + 8 * half
            message = jnp.zeros((8, LANES), F32)
            for lev, m in enumerate((1, 2, 4, 8)):
                reach = (target // (2 * m) == me // (2 * m)) & (target // m == me // m + 1)
                message = jnp.where(reach, levels[lev], message)
            send_ref[8 * half : 8 * half + 8, lanes] = message


def outflow(me, out, t1, t2, t4):
    return pl.pallas_call(
        outflow_kernel,
        in_specs=[SMEM] + [VMEM] * 4,
        out_specs=VMEM,
        out_shape=jax.ShapeDtypeStruct((16, 256), F32),
        compiler_params=pltpu.CompilerParams(vmem_limit_bytes=4 << 20),
        name="outflow",
    )(me, out, t1, t2, t4)


def finish_kernel(me_ref, got_ref, g_ref, t1_ref, t2_ref, t4_ref, spike_ref, out_ref, raw):
    n = g_ref.shape[0]
    blocks = n // SPAN
    me = me_ref[0]
    source = iota((16, LANES), 0)
    pairs = []
    for p in range(2):
        lanes = slice(LANES * p, LANES * (p + 1))
        got = got_ref[:, lanes]
        v = None
        for m, t_ref in ((8, None), (4, t4_ref), (2, t2_ref), (1, t1_ref)):
            from_here = (source // (2 * m) == me // (2 * m)) & (source // m + 1 == me // m)
            part = jnp.sum(jnp.where(from_here, got, 0.0), axis=0, keepdims=True)
            part = jnp.broadcast_to(part, (8, LANES))
            if v is None:
                v = part
            else:
                moved = times_map(v, split(expand(t_ref[...])[p]))
                v = jnp.where((me // m) % 2 == 1, moved, v) + part
        pairs.append(v)
    row, lane = iota((8, LANES), 0), iota((8, LANES), 1)

    def lines_of(pair):
        rows = [line_rows(pair[l // 2], l // 2, l % 2) for l in range(4)]
        x = rows[0]
        for l in range(1, 4):
            x = jnp.where(row % 4 == l, rows[l], x)
        return x

    sums, own = reduce_lanes(), own_lane()
    x = lines_of(pairs)
    step = 2
    for b in range(blocks):
        lhs = both(jnp.where(row // 4 == lane // WIDTH, x, 0.0))
        if b + 1 < blocks:
            e = SPAN * b + SPAN - 1
            last = [
                jnp.broadcast_to(g_ref[e : e + 1, LANES * p : LANES * (p + 1)], (8, LANES))
                for p in range(2)
            ]
            x = lying_matvec(x, spike_ref[e], sums, own) + lines_of(last)
        for k in range(0, SPAN, step):
            e = SPAN * b + k
            y = fold(dot_t(lhs, spike_ref[e : e + step].reshape(step * LANES, LANES)))
            for t in range(step):
                raw[8 * (e + t) : 8 * (e + t) + 8, :] = y[:, LANES * t : LANES * (t + 1)]
    lane_n = iota((n, LANES), 1)
    parts = []
    for a in range(2):
        acc = jnp.zeros((n, LANES), F32)
        for l in range(4):
            acc = jnp.where(lane_n % 4 == l, raw[pl.ds(4 * a + l, n, stride=8), :], acc)
        parts.append(acc)
    y = jnp.concatenate(parts, axis=1)
    src, dst = iota((256, 256), 0), iota((256, 256), 1)
    want = LANES * (dst % 2) + 4 * ((dst % WIDTH) // 2) + dst // WIDTH
    order = jnp.where(src == want, 1.0, 0.0).astype(BF16)
    high, rest = split(y)
    out_ref[...] = dot(high, order) + dot(rest, order) + g_ref[...]


def finish(me, got, g, t1, t2, t4, spike):
    n = g.shape[0]
    vmem = pl.BlockSpec(memory_space=pltpu.VMEM)
    return pl.pallas_call(
        finish_kernel,
        in_specs=[pl.BlockSpec(memory_space=pltpu.SMEM)] + [vmem] * 6,
        out_specs=vmem,
        out_shape=jax.ShapeDtypeStruct((n, 256), F32),
        scratch_shapes=[pltpu.VMEM((8 * n, LANES), F32)],
        compiler_params=pltpu.CompilerParams(vmem_limit_bytes=4 << 20),
        name="finish",
    )(me, got, g, t1, t2, t4, spike)


def flip(x, axis, bit):
    count = lax.axis_size(axis)
    return lax.ppermute(x, axis, [(i, i ^ bit) for i in range(count)])


def between(x, axis):
    count = lax.axis_size(axis)
    pairs = [(i, i + 1) for i in range(1, count - 1, 2)]
    return lax.ppermute(x, axis, pairs + [(j, i) for i, j in pairs])


def on_device(rhs, previous, dinv, lower, spike, coupling, nbr_line, nbr_shift):
    n = rhs.shape[0]
    stream, cross = lax.axis_index("stream"), lax.axis_index("cross")
    me = stream.reshape(1)

    def as_it_lies(x):
        return x.reshape(n, 4, 32, LANES).transpose(0, 2, 1, 3).reshape(n, LANES, LANES)

    far = between(previous, "cross")
    near = flip(previous, "cross", 1)
    low = jnp.where(cross % 2 == 0, far, near)
    high = jnp.where(cross % 2 == 0, near, far)
    even = stream % 2 == 0
    first = jnp.concatenate([low[:1], high[:1]], axis=0)
    last = jnp.concatenate([low[n - 1 :], high[n - 1 :]], axis=0)
    to_mate, to_beyond = jnp.where(even, last, first), jnp.where(even, first, last)
    spike_x = as_it_lies(spike)
    own1 = device_map(spike_x)
    t1 = flip(own1, "stream", 1)
    beyond = between(to_beyond, "stream")
    mate = flip(to_mate, "stream", 1)
    mate, own1, t1 = lax.optimization_barrier((mate, own1, t1))
    edge = jnp.concatenate([jnp.where(even, beyond, mate), jnp.where(even, mate, beyond)], axis=0)
    own2 = product(me % 2, own1, t1)
    t2 = flip(own2, "stream", 2)
    low, own2 = lax.optimization_barrier((low, own2))

    line = cross * 4 + lax.broadcasted_iota(jnp.int32, nbr_line.shape, 1)
    code = (jnp.where(nbr_line > line, 3, 0) + nbr_shift).astype(F32)
    code = code.transpose(1, 2, 0).reshape(8, n)
    coupling_x = (
        coupling.reshape(n, 4, 2, 32, LANES).transpose(0, 1, 3, 2, 4).reshape(n, 256, LANES)
    )
    res, ends, ends_coupling, lower_v, dinv_v = residual(
        code, low, high, rhs, coupling_x, as_it_lies(lower), as_it_lies(dinv)
    )
    res, own2, t2 = lax.optimization_barrier((res, own2, t2))
    own4 = product((me // 2) % 2, own2, t2)
    t4 = flip(own4, "stream", 4)
    g, out = chain(res, ends, edge, ends_coupling, lower_v, dinv_v, spike_x)
    send = outflow(me, out, t1, t2, t4)
    got = lax.all_to_all(send, "stream", 0, 0, tiled=True)
    return finish(me, got, g, t1, t2, t4, spike_x)


def solution(mesh):
    return jax.shard_map(
        on_device,
        mesh=mesh,
        in_specs=(
            P("stream", "cross"),
            P("stream", "cross"),
            P("stream", "cross", None),
            P("stream", "cross", None),
            P("stream", "cross", None),
            P("stream", "cross", None, None),
            P("stream", "cross", None),
            P("stream", "cross", None),
        ),
        out_specs=P("stream", "cross"),
        check_vma=False,
    )
```

```python
import functools

import jax
import jax.numpy as jnp
from jax import lax
from jax.experimental import pallas as pl
from jax.experimental.pallas import tpu as pltpu
from jax.sharding import PartitionSpec as P

WIDTH = 64
SPAN = 16
LANES = 128
F32 = jnp.float32
BF16 = jnp.bfloat16


def iota(shape, dim):
    return lax.broadcasted_iota(jnp.int32, shape, dim)


def swap_halves(x):
    return jnp.concatenate([x[:, WIDTH:], x[:, :WIDTH]], axis=1)


def dot(a, b):
    return jnp.dot(a, b, preferred_element_type=F32)


def dot_t(a, b):
    return lax.dot_general(a, b, (((1,), (1,)), ((), ())), preferred_element_type=F32)


def split(x):
    high = x.astype(BF16)
    return high, (x - high.astype(F32)).astype(BF16)


def both(x):
    high = x.astype(BF16).astype(F32)
    return jnp.concatenate([high, x - high], axis=0).astype(BF16)


def fold(y):
    return y[:8] + y[8:]


def order_rows():
    row, col = iota((256, 256), 0), iota((256, 256), 1)
    line, i = row // WIDTH, row % WIDTH
    swapped = (i % 2) != (line % 2)
    want = 4 * (i // 2) + line + jnp.where(swapped, LANES, 0)
    return jnp.where(col == want, 1.0, 0.0).astype(BF16)


def half_mask(rows):
    return (iota((rows, LANES), 0) // WIDTH) % 2 == iota((rows, LANES), 1) // WIDTH


def paired(x, order):
    both_ways = jnp.concatenate([x, swap_halves(x)], axis=0)
    y = dot(order, both_ways)
    return jnp.where(half_mask(256), y, 0.0).astype(BF16)


def expand(c):
    s = swap_halves(c)
    low = iota(c.shape, 1) < WIDTH
    mask = half_mask(LANES)
    return (
        jnp.where(mask, jnp.where(low, c, s), 0.0),
        jnp.where(mask, jnp.where(low, s, c), 0.0),
    )


def device_map_kernel(spike_hbm, out_ref, after_ref, spike_v, sems):
    blocks = spike_v.shape[0]
    copies = [
        pltpu.make_async_copy(spike_hbm.at[SPAN * b + SPAN - 1], spike_v.at[b], sems.at[b])
        for b in range(blocks)
    ]
    for c in copies:
        c.start()
    order = order_rows()
    low = iota((LANES, LANES), 1) < WIDTH
    total = None
    for b in range(blocks - 1, -1, -1):
        copies[b].wait()
        m = paired(spike_v[b], order)
        m0, m1 = m[:LANES].astype(F32), m[LANES:].astype(F32)
        c = jnp.where(low, m0 + swap_halves(m0), m1 + swap_halves(m1))
        if total is None:
            total = c
        else:
            before, parts = c.astype(BF16), []
            for after in expand(total):
                high, rest = split(after)
                parts.append(dot(high, before) + dot(rest, before))
            total = jnp.where(low, parts[0], parts[1])
        if b > 0:
            after_ref[b - 1] = total
    out_ref[...] = total


ALMOST_ALL = 53 << 20
MOST = 49 << 20
VMEM = pl.BlockSpec(memory_space=pltpu.VMEM)
SMEM = pl.BlockSpec(memory_space=pltpu.SMEM)
HBM = pl.BlockSpec(memory_space=pltpu.HBM)


def device_map(spike):
    blocks = spike.shape[0] // SPAN
    return pl.pallas_call(
        device_map_kernel,
        in_specs=[HBM],
        out_specs=[VMEM] * 2,
        out_shape=[
            jax.ShapeDtypeStruct((LANES, LANES), F32),
            jax.ShapeDtypeStruct((blocks - 1, LANES, LANES), F32),
        ],
        scratch_shapes=[
            pltpu.VMEM((blocks, LANES, LANES), BF16),
            pltpu.SemaphoreType.DMA((blocks,)),
        ],
        compiler_params=pltpu.CompilerParams(vmem_limit_bytes=ALMOST_ALL),
        name="device_map",
    )(spike)


def multiply(upper_ref, own_ref, other_ref):
    upper = upper_ref[0] > 0
    own, other = own_ref[...], other_ref[...]
    after = jnp.where(upper, own, other)
    before_h, before_l = split(jnp.where(upper, other, own))
    low = iota((LANES, LANES), 1) < WIDTH
    parts = []
    for m in expand(after):
        high, rest = split(m)
        parts.append(dot(high, before_h) + dot(rest, before_h) + dot(high, before_l))
    return jnp.where(low, parts[0], parts[1])


def product_kernel(upper_ref, own_ref, other_ref, out_ref):
    out_ref[...] = multiply(upper_ref, own_ref, other_ref)


def product(upper, own, other):
    return pl.pallas_call(
        product_kernel,
        in_specs=[
            pl.BlockSpec(memory_space=pltpu.SMEM),
            pl.BlockSpec(memory_space=pltpu.VMEM),
            pl.BlockSpec(memory_space=pltpu.VMEM),
        ],
        out_specs=pl.BlockSpec(memory_space=pltpu.VMEM),
        out_shape=jax.ShapeDtypeStruct((LANES, LANES), F32),
        compiler_params=pltpu.CompilerParams(vmem_limit_bytes=4 << 20),
        name="product",
    )(upper, own, other)


def times_map(x, c_parts):
    lhs = both(x)
    high, rest = c_parts
    return fold(dot_t(lhs, high)) + dot_t(lhs, rest)[:8]


def reduce_lanes():
    row, col = iota((256, LANES), 0), iota((256, LANES), 1)
    return jnp.where(col % 2 == (row % LANES) // WIDTH, 1.0, 0.0).astype(BF16)


def own_lane():
    return iota((LANES, LANES), 0) // 4 == (iota((LANES, LANES), 1) % WIDTH) // 2


def lying_matvec(x, m, sums, own):
    prod = (m.astype(F32).reshape(16, 8, LANES) * x[None]).reshape(LANES, LANES)
    high = prod.astype(BF16)
    rest = (prod - high.astype(F32)).astype(BF16)
    z = dot(jnp.concatenate([high, rest], axis=1), sums)
    z = jnp.sum(jnp.where(own, z, 0.0).reshape(16, 8, LANES), axis=0)
    return z + pltpu.roll(z, 4, 0)


def line_rows(natural, p, q):
    lane = iota(natural.shape, 1)
    return jnp.where(lane // WIDTH == q, natural, swap_halves(natural))


def look_up(code_ref):
    code = code_ref[...].astype(BF16)
    r8, c8 = iota((8, 512), 0), iota((8, 512), 1)
    spread = jnp.where((r8 // 2 == (c8 % 256) // WIDTH) & (r8 % 2 == c8 // 256), 1.0, 0.0)
    return lax.dot_general(
        code, spread.astype(BF16), (((0,), (0,)), ((), ())), preferred_element_type=F32
    )


def residual_rows(n, where, rows_at, rhs, blocks_of, vec, raw):
    lane = iota((n, LANES), 1)
    for f in range(2):
        for p in range(2):
            w = where[:, 256 * f + LANES * p : 256 * f + LANES * (p + 1)]
            x = jnp.zeros((n, LANES), F32)
            for side in range(2):
                for s in range(3):
                    x = jnp.where(w == float(3 * side + s), rows_at(side, s, p), x)
            top = x.astype(BF16).astype(F32)
            for h, part in enumerate((top, x - top)):
                turned = swap_halves(part)
                for q in range(2):
                    for a in range(2):
                        v = jnp.where(lane // WIDTH == a, part if a == q else turned, 0.0)
                        vec[2 * p + h, pl.ds(4 * q + 2 * f + a, n, stride=8), :] = v

    for t, blocks in blocks_of:
        for p in range(2):
            lhs = jnp.concatenate(
                [vec[2 * p, 8 * t : 8 * t + 8, :], vec[2 * p + 1, 8 * t : 8 * t + 8, :]], axis=0
            ).astype(BF16)
            raw[p, 8 * t : 8 * t + 8, :] = fold(dot_t(lhs, blocks(p)))
    even = lane % 2 == 0
    lines = []
    for p in range(2):
        y = None
        for a in range(2):
            acc = jnp.zeros((n, LANES), F32)
            for q in range(2):
                for f in range(2):
                    z = raw[p, pl.ds(4 * q + 2 * f + a, n, stride=8), :]
                    acc = jnp.where((lane // WIDTH == q) & (lane % 2 == f), z, acc)
            acc = acc + jnp.where(even, pltpu.roll(acc, LANES - 1, 1), pltpu.roll(acc, 1, 1))
            y = acc if a == 0 else jnp.where(even, y, acc)
        residual = rhs[:, LANES * p : LANES * (p + 1)] - y
        for q in range(2):
            lines.append((2 * p + q, line_rows(residual, p, q)))
    return lines


def residual_kernel(code_ref, low_ref, high_ref, rhs_ref, coupling_hbm, lower_hbm, dinv_hbm, *rest):
    res, ends_ref, ends_coupling, lower_v, dinv_v, coupling_v, sides, vec, raw, sems = rest
    n = rhs_ref.shape[0]
    cuts = [0, n // 8, n // 4, n // 2, n]
    copies = {
        lo: pltpu.make_async_copy(
            coupling_hbm.at[pl.ds(lo, hi - lo)], coupling_v.at[pl.ds(lo, hi - lo)], sems.at[i]
        )
        for i, (lo, hi) in enumerate(zip(cuts, cuts[1:]))
    }
    later = [
        pltpu.make_async_copy(lower_hbm, lower_v, sems.at[4]),
        pltpu.make_async_copy(dinv_hbm, dinv_v, sems.at[5]),
    ]
    for c in list(copies.values()) + later:
        c.start()
    where = look_up(code_ref)
    ends_ref[0:1, :] = where[0:1]
    ends_ref[1:2, :] = where[n - 1 : n]
    for side, ref in enumerate((low_ref, high_ref)):
        sides[side, 0:8, :] = jnp.zeros((8, 256), F32)
        sides[side, 8 : n + 8, :] = ref[...]
        sides[side, n + 8 : n + 16, :] = jnp.zeros((8, 256), F32)

    def rows_at(side, s, p):
        return sides[side, pl.ds(7 + s, n), LANES * p : LANES * (p + 1)]

    def blocks_of():
        for e in range(n):
            if e in copies:
                copies[e].wait()
            yield e, lambda p: coupling_v[e, LANES * p : LANES * (p + 1), :]

    for line, rows in residual_rows(n, where, rows_at, rhs_ref[...], blocks_of(), vec, raw):
        res[pl.ds(line, n, stride=8), :] = rows
        res[pl.ds(line + 4, n, stride=8), :] = rows
    ends_coupling[0] = coupling_v[0]
    ends_coupling[1] = coupling_v[n - 1]
    for c in later:
        c.wait()


def residual(code, low, high, rhs, coupling, lower, dinv):
    n = rhs.shape[0]
    return pl.pallas_call(
        residual_kernel,
        in_specs=[VMEM] * 4 + [HBM] * 3,
        out_specs=[VMEM] * 5,
        out_shape=[
            jax.ShapeDtypeStruct((8 * n, LANES), F32),
            jax.ShapeDtypeStruct((2, 512), F32),
            jax.ShapeDtypeStruct((2, 256, LANES), BF16),
            jax.ShapeDtypeStruct(lower.shape, BF16),
            jax.ShapeDtypeStruct(dinv.shape, BF16),
        ],
        scratch_shapes=[
            pltpu.VMEM((n, 256, LANES), BF16),
            pltpu.VMEM((2, n + 16, 256), F32),
            pltpu.VMEM((4, 8 * n, LANES), F32),
            pltpu.VMEM((2, 8 * n, LANES), F32),
            pltpu.SemaphoreType.DMA((6,)),
        ],
        compiler_params=pltpu.CompilerParams(vmem_limit_bytes=MOST),
        cost_estimate=pl.CostEstimate(flops=10**8, bytes_accessed=4 << 20, transcendentals=0),
        name="residual",
    )(code, low, high, rhs, coupling, lower, dinv)


def edge_terms(t, code, edge, blocks):
    row, lane = iota((8, LANES), 0), iota((8, LANES), 1)
    q, f, a = row // 4, (row // 2) % 2, row % 2
    lines = jnp.zeros((8, LANES), F32)
    for p in range(2):
        lanes = slice(LANES * p, LANES * (p + 1))
        below = jnp.broadcast_to(edge[2 * t : 2 * t + 1, lanes], (8, LANES))
        above = jnp.broadcast_to(edge[2 * t + 1 : 2 * t + 2, lanes], (8, LANES))
        w = jnp.where(f == 0, code[t : t + 1, lanes], code[t : t + 1, 256 + LANES * p : 256 + LANES * (p + 1)])
        x = jnp.where(w == 2.0 * t, below, jnp.where(w == 3.0 + 2.0 * t, above, 0.0))
        x = jnp.where(lane // WIDTH == a, jnp.where(a == q, x, swap_halves(x)), 0.0)
        y = fold(dot_t(both(x), blocks(p)))
        y = jnp.where((lane // WIDTH == q) & (lane % 2 == f), y, 0.0)
        y = y + jnp.where(lane % 2 == 0, pltpu.roll(y, LANES - 1, 1), pltpu.roll(y, 1, 1))
        y = jnp.sum(jnp.where(lane % 2 == a, y, 0.0), axis=0, keepdims=True)
        y = jnp.broadcast_to(y, (8, LANES))
        for h in range(2):
            lines = jnp.where(row % 4 == 2 * p + h, line_rows(y, p, h), lines)
    return lines


def product_and_edges_kernel(
    upper_ref, own_ref, other_ref, ends_ref, edge_ref, coupling_ref, out_ref, terms_ref
):
    out_ref[...] = multiply(upper_ref, own_ref, other_ref)
    code, edge = ends_ref[...], edge_ref[...]
    for t in range(2):
        terms_ref[t] = edge_terms(t, code, edge, lambda p: coupling_ref[t, LANES * p : LANES * (p + 1), :])


def product_and_edges(upper, own, other, ends, edge, coupling):
    return pl.pallas_call(
        product_and_edges_kernel,
        in_specs=[SMEM] + [VMEM] * 5,
        out_specs=[VMEM] * 2,
        out_shape=[
            jax.ShapeDtypeStruct((LANES, LANES), F32),
            jax.ShapeDtypeStruct((2, 8, LANES), F32),
        ],
        compiler_params=pltpu.CompilerParams(vmem_limit_bytes=4 << 20),
        name="product_and_edges",
    )(upper, own, other, ends, edge, coupling)


def chain_kernel(res, terms_ref, lower_ref, dinv_ref, sol):
    n = lower_ref.shape[0]
    blocks = n // SPAN
    ends = (0, n - 1)
    sums, own = reduce_lanes(), own_lane()
    g = [None] * blocks
    for k in range(SPAN):
        for b in range(blocks):
            e = SPAN * b + k
            balance = res[8 * e : 8 * e + 8, :]
            if e in ends:
                balance = balance - terms_ref[ends.index(e)]
            if k > 0:
                balance = balance - lying_matvec(g[b], lower_ref[e], sums, own)
            g[b] = lying_matvec(balance, dinv_ref[e], sums, own)
            sol[8 * e : 8 * e + 8, :] = g[b]


def chain(res, terms, lower, dinv):
    n = lower.shape[0]
    return pl.pallas_call(
        chain_kernel,
        in_specs=[VMEM] * 4,
        out_specs=VMEM,
        out_shape=jax.ShapeDtypeStruct((8 * n, LANES), F32),
        compiler_params=pltpu.CompilerParams(vmem_limit_bytes=MOST),
        cost_estimate=pl.CostEstimate(flops=10**9, bytes_accessed=4 << 20, transcendentals=0),
        name="chain",
    )(res, terms, lower, dinv)


def outflow_kernel(me_ref, sol, after_ref, t1_ref, t2_ref, t4_ref, g_ref, send_ref):
    me = me_ref[0]
    n = g_ref.shape[0]
    blocks = n // SPAN
    lane = iota((n, LANES), 1)
    for p in range(2):
        lanes = slice(LANES * p, LANES * (p + 1))
        g = jnp.where(
            lane < WIDTH, sol[pl.ds(2 * p, n, stride=8), :], sol[pl.ds(2 * p + 1, n, stride=8), :]
        )
        g_ref[:, lanes] = g
        w = None
        for b in range(blocks - 1, -1, -1):
            e = SPAN * b + SPAN - 1
            last = jnp.broadcast_to(g[e : e + 1], (8, LANES))
            if b < blocks - 1:
                last = times_map(last, split(expand(after_ref[b])[p]))
            w = last if w is None else w + last
        levels = [w]
        for m, t_ref in ((1, t1_ref), (2, t2_ref), (4, t4_ref)):
            moved = times_map(w, split(expand(t_ref[...])[p]))
            w = jnp.where((me // m) % 2 == 0, moved, w)
            levels.append(w)
        for half in range(2):
            target = iota((8, LANES), 0) + 8 * half
            message = jnp.zeros((8, LANES), F32)
            for lev, m in enumerate((1, 2, 4, 8)):
                reach = (target // (2 * m) == me // (2 * m)) & (target // m == me // m + 1)
                message = jnp.where(reach, levels[lev], message)
            send_ref[8 * half : 8 * half + 8, lanes] = message


def outflow(me, sol, after, t1, t2, t4):
    n = sol.shape[0] // 8
    return pl.pallas_call(
        outflow_kernel,
        in_specs=[SMEM] + [VMEM] * 5,
        out_specs=[VMEM] * 2,
        out_shape=[
            jax.ShapeDtypeStruct((n, 256), F32),
            jax.ShapeDtypeStruct((16, 256), F32),
        ],
        compiler_params=pltpu.CompilerParams(vmem_limit_bytes=4 << 20),
        name="outflow",
    )(me, sol, after, t1, t2, t4)


def finish_kernel(me_ref, got_ref, g_ref, t1_ref, t2_ref, t4_ref, spike_ref, out_ref, raw):
    n = g_ref.shape[0]
    blocks = n // SPAN
    me = me_ref[0]
    source = iota((16, LANES), 0)
    pairs = []
    for p in range(2):
        lanes = slice(LANES * p, LANES * (p + 1))
        got = got_ref[:, lanes]
        v = None
        for m, t_ref in ((8, None), (4, t4_ref), (2, t2_ref), (1, t1_ref)):
            from_here = (source // (2 * m) == me // (2 * m)) & (source // m + 1 == me // m)
            part = jnp.sum(jnp.where(from_here, got, 0.0), axis=0, keepdims=True)
            part = jnp.broadcast_to(part, (8, LANES))
            if v is None:
                v = part
            else:
                moved = times_map(v, split(expand(t_ref[...])[p]))
                v = jnp.where((me // m) % 2 == 1, moved, v) + part
        pairs.append(v)
    row, lane = iota((8, LANES), 0), iota((8, LANES), 1)

    def lines_of(pair):
        rows = [line_rows(pair[l // 2], l // 2, l % 2) for l in range(4)]
        x = rows[0]
        for l in range(1, 4):
            x = jnp.where(row % 4 == l, rows[l], x)
        return x

    sums, own = reduce_lanes(), own_lane()
    x = lines_of(pairs)
    step = 2
    for b in range(blocks):
        lhs = both(jnp.where(row // 4 == lane // WIDTH, x, 0.0))
        if b + 1 < blocks:
            e = SPAN * b + SPAN - 1
            last = [
                jnp.broadcast_to(g_ref[e : e + 1, LANES * p : LANES * (p + 1)], (8, LANES))
                for p in range(2)
            ]
            x = lying_matvec(x, spike_ref[e], sums, own) + lines_of(last)
        for k in range(0, SPAN, step):
            e = SPAN * b + k
            y = fold(dot_t(lhs, spike_ref[e : e + step].reshape(step * LANES, LANES)))
            for t in range(step):
                raw[8 * (e + t) : 8 * (e + t) + 8, :] = y[:, LANES * t : LANES * (t + 1)]
    lane_n = iota((n, LANES), 1)
    parts = []
    for a in range(2):
        acc = jnp.zeros((n, LANES), F32)
        for l in range(4):
            acc = jnp.where(lane_n % 4 == l, raw[pl.ds(4 * a + l, n, stride=8), :], acc)
        parts.append(acc)
    y = jnp.concatenate(parts, axis=1)
    src, dst = iota((256, 256), 0), iota((256, 256), 1)
    want = LANES * (dst % 2) + 4 * ((dst % WIDTH) // 2) + dst // WIDTH
    order = jnp.where(src == want, 1.0, 0.0).astype(BF16)
    high, rest = split(y)
    out_ref[...] = dot(high, order) + dot(rest, order) + g_ref[...]


def finish(me, got, g, t1, t2, t4, spike):
    n = g.shape[0]
    vmem = pl.BlockSpec(memory_space=pltpu.VMEM)
    return pl.pallas_call(
        finish_kernel,
        in_specs=[pl.BlockSpec(memory_space=pltpu.SMEM)] + [vmem] * 6,
        out_specs=vmem,
        out_shape=jax.ShapeDtypeStruct((n, 256), F32),
        scratch_shapes=[pltpu.VMEM((8 * n, LANES), F32)],
        compiler_params=pltpu.CompilerParams(vmem_limit_bytes=4 << 20),
        name="finish",
    )(me, got, g, t1, t2, t4, spike)


def flip(x, axis, bit):
    count = lax.axis_size(axis)
    return lax.ppermute(x, axis, [(i, i ^ bit) for i in range(count)])


def between(x, axis):
    count = lax.axis_size(axis)
    pairs = [(i, i + 1) for i in range(1, count - 1, 2)]
    return lax.ppermute(x, axis, pairs + [(j, i) for i, j in pairs])


def on_device(rhs, previous, dinv, lower, spike, coupling, nbr_line, nbr_shift):
    n = rhs.shape[0]
    stream, cross = lax.axis_index("stream"), lax.axis_index("cross")
    me = stream.reshape(1)

    def as_it_lies(x):
        return x.reshape(n, 4, 32, LANES).transpose(0, 2, 1, 3).reshape(n, LANES, LANES)

    far = between(previous, "cross")
    near = flip(previous, "cross", 1)
    low = jnp.where(cross % 2 == 0, far, near)
    high = jnp.where(cross % 2 == 0, near, far)
    even = stream % 2 == 0
    first = jnp.concatenate([low[:1], high[:1]], axis=0)
    last = jnp.concatenate([low[n - 1 :], high[n - 1 :]], axis=0)
    to_mate, to_beyond = jnp.where(even, last, first), jnp.where(even, first, last)
    spike_x = as_it_lies(spike)
    own1, after = device_map(spike_x)
    t1 = flip(own1, "stream", 1)
    beyond = between(to_beyond, "stream")
    mate = flip(to_mate, "stream", 1)
    own2 = product(me % 2, own1, t1)
    mate, own2 = lax.optimization_barrier((mate, own2))
    edge = jnp.concatenate([jnp.where(even, beyond, mate), jnp.where(even, mate, beyond)], axis=0)
    t2 = flip(own2, "stream", 2)
    low, own2 = lax.optimization_barrier((low, own2))

    line = cross * 4 + lax.broadcasted_iota(jnp.int32, nbr_line.shape, 1)
    code = (jnp.where(nbr_line > line, 3, 0) + nbr_shift).astype(F32)
    code = code.transpose(1, 2, 0).reshape(8, n)
    coupling_x = (
        coupling.reshape(n, 4, 2, 32, LANES).transpose(0, 1, 3, 2, 4).reshape(n, 256, LANES)
    )
    res, ends, ends_coupling, lower_v, dinv_v = residual(
        code, low, high, rhs, coupling_x, as_it_lies(lower), as_it_lies(dinv)
    )
    res, own2, t2 = lax.optimization_barrier((res, own2, t2))
    own4, terms = product_and_edges((me // 2) % 2, own2, t2, ends, edge, ends_coupling)
    t4 = flip(own4, "stream", 4)
    sol = chain(res, terms, lower_v, dinv_v)
    g, send = outflow(me, sol, after, t1, t2, t4)
    got = lax.all_to_all(send, "stream", 0, 0, tiled=True)
    return finish(me, got, g, t1, t2, t4, spike_x)


def solution(mesh):
    return jax.shard_map(
        on_device,
        mesh=mesh,
        in_specs=(
            P("stream", "cross"),
            P("stream", "cross"),
            P("stream", "cross", None),
            P("stream", "cross", None),
            P("stream", "cross", None),
            P("stream", "cross", None, None),
            P("stream", "cross", None),
            P("stream", "cross", None),
        ),
        out_specs=P("stream", "cross"),
        check_vma=False,
    )
```

```python
import functools

import jax
import jax.numpy as jnp
from jax import lax
from jax.experimental import pallas as pl
from jax.experimental.pallas import tpu as pltpu
from jax.sharding import PartitionSpec as P

WIDTH = 64
SPAN = 16
LANES = 128
F32 = jnp.float32
BF16 = jnp.bfloat16


def iota(shape, dim):
    return lax.broadcasted_iota(jnp.int32, shape, dim)


def swap_halves(x):
    return jnp.concatenate([x[:, WIDTH:], x[:, :WIDTH]], axis=1)


def dot(a, b):
    return jnp.dot(a, b, preferred_element_type=F32)


def dot_t(a, b):
    return lax.dot_general(a, b, (((1,), (1,)), ((), ())), preferred_element_type=F32)


def split(x):
    high = x.astype(BF16)
    return high, (x - high.astype(F32)).astype(BF16)


def both(x):
    high = x.astype(BF16).astype(F32)
    return jnp.concatenate([high, x - high], axis=0).astype(BF16)


def fold(y):
    return y[:8] + y[8:]


def order_rows():
    row, col = iota((256, 256), 0), iota((256, 256), 1)
    line, i = row // WIDTH, row % WIDTH
    swapped = (i % 2) != (line % 2)
    want = 4 * (i // 2) + line + jnp.where(swapped, LANES, 0)
    return jnp.where(col == want, 1.0, 0.0).astype(BF16)


def half_mask(rows):
    return (iota((rows, LANES), 0) // WIDTH) % 2 == iota((rows, LANES), 1) // WIDTH


def paired(x, order):
    both_ways = jnp.concatenate([x, swap_halves(x)], axis=0)
    y = dot(order, both_ways)
    return jnp.where(half_mask(256), y, 0.0).astype(BF16)


def expand(c):
    s = swap_halves(c)
    low = iota(c.shape, 1) < WIDTH
    mask = half_mask(LANES)
    return (
        jnp.where(mask, jnp.where(low, c, s), 0.0),
        jnp.where(mask, jnp.where(low, s, c), 0.0),
    )


def device_map_kernel(spike_hbm, out_ref, after_ref, spike_v, sems):
    blocks = spike_v.shape[0]
    copies = [
        pltpu.make_async_copy(spike_hbm.at[SPAN * b + SPAN - 1], spike_v.at[b], sems.at[b])
        for b in range(blocks)
    ]
    for c in copies:
        c.start()
    order = order_rows()
    low = iota((LANES, LANES), 1) < WIDTH
    total = None
    for b in range(blocks - 1, -1, -1):
        copies[b].wait()
        m = paired(spike_v[b], order)
        m0, m1 = m[:LANES].astype(F32), m[LANES:].astype(F32)
        c = jnp.where(low, m0 + swap_halves(m0), m1 + swap_halves(m1))
        if total is None:
            total = c
        else:
            before, parts = c.astype(BF16), []
            for after in expand(total):
                high, rest = split(after)
                parts.append(dot(high, before) + dot(rest, before))
            total = jnp.where(low, parts[0], parts[1])
        if b > 0:
            after_ref[b - 1] = total
    out_ref[...] = total


ALMOST_ALL = 53 << 20
MOST = 49 << 20
VMEM = pl.BlockSpec(memory_space=pltpu.VMEM)
SMEM = pl.BlockSpec(memory_space=pltpu.SMEM)
HBM = pl.BlockSpec(memory_space=pltpu.HBM)


def device_map(spike):
    blocks = spike.shape[0] // SPAN
    return pl.pallas_call(
        device_map_kernel,
        in_specs=[HBM],
        out_specs=[VMEM] * 2,
        out_shape=[
            jax.ShapeDtypeStruct((LANES, LANES), F32),
            jax.ShapeDtypeStruct((blocks - 1, LANES, LANES), F32),
        ],
        scratch_shapes=[
            pltpu.VMEM((blocks, LANES, LANES), BF16),
            pltpu.SemaphoreType.DMA((blocks,)),
        ],
        compiler_params=pltpu.CompilerParams(vmem_limit_bytes=ALMOST_ALL),
        name="device_map",
    )(spike)


def multiply(upper_ref, own_ref, other_ref):
    upper = upper_ref[0] > 0
    own, other = own_ref[...], other_ref[...]
    after = jnp.where(upper, own, other)
    before_h, before_l = split(jnp.where(upper, other, own))
    low = iota((LANES, LANES), 1) < WIDTH
    parts = []
    for m in expand(after):
        high, rest = split(m)
        parts.append(dot(high, before_h) + dot(rest, before_h) + dot(high, before_l))
    return jnp.where(low, parts[0], parts[1])


def product_kernel(upper_ref, own_ref, other_ref, out_ref):
    out_ref[...] = multiply(upper_ref, own_ref, other_ref)


def product(upper, own, other):
    return pl.pallas_call(
        product_kernel,
        in_specs=[
            pl.BlockSpec(memory_space=pltpu.SMEM),
            pl.BlockSpec(memory_space=pltpu.VMEM),
            pl.BlockSpec(memory_space=pltpu.VMEM),
        ],
        out_specs=pl.BlockSpec(memory_space=pltpu.VMEM),
        out_shape=jax.ShapeDtypeStruct((LANES, LANES), F32),
        compiler_params=pltpu.CompilerParams(vmem_limit_bytes=4 << 20),
        name="product",
    )(upper, own, other)


def times_map(x, c_parts):
    lhs = both(x)
    high, rest = c_parts
    return fold(dot_t(lhs, high)) + dot_t(lhs, rest)[:8]


def reduce_lanes():
    row, col = iota((256, LANES), 0), iota((256, LANES), 1)
    return jnp.where(col % 2 == (row % LANES) // WIDTH, 1.0, 0.0).astype(BF16)


def own_lane():
    return iota((LANES, LANES), 0) // 4 == (iota((LANES, LANES), 1) % WIDTH) // 2


def lying_matvec(x, m, sums, own):
    prod = (m.astype(F32).reshape(16, 8, LANES) * x[None]).reshape(LANES, LANES)
    high = prod.astype(BF16)
    rest = (prod - high.astype(F32)).astype(BF16)
    z = dot(jnp.concatenate([high, rest], axis=1), sums)
    z = jnp.sum(jnp.where(own, z, 0.0).reshape(16, 8, LANES), axis=0)
    return z + pltpu.roll(z, 4, 0)


def line_rows(natural, p, q):
    lane = iota(natural.shape, 1)
    return jnp.where(lane // WIDTH == q, natural, swap_halves(natural))


def look_up(code_ref):
    code = code_ref[...].astype(BF16)
    r8, c8 = iota((8, 512), 0), iota((8, 512), 1)
    spread = jnp.where((r8 // 2 == (c8 % 256) // WIDTH) & (r8 % 2 == c8 // 256), 1.0, 0.0)
    return lax.dot_general(
        code, spread.astype(BF16), (((0,), (0,)), ((), ())), preferred_element_type=F32
    )


def residual_rows(n, where, rows_at, rhs, blocks_of, vec, raw):
    lane = iota((n, LANES), 1)
    for f in range(2):
        for p in range(2):
            w = where[:, 256 * f + LANES * p : 256 * f + LANES * (p + 1)]
            x = jnp.zeros((n, LANES), F32)
            for side in range(2):
                for s in range(3):
                    x = jnp.where(w == float(3 * side + s), rows_at(side, s, p), x)
            top = x.astype(BF16).astype(F32)
            for h, part in enumerate((top, x - top)):
                turned = swap_halves(part)
                for q in range(2):
                    for a in range(2):
                        v = jnp.where(lane // WIDTH == a, part if a == q else turned, 0.0)
                        vec[2 * p + h, pl.ds(4 * q + 2 * f + a, n, stride=8), :] = v

    for t, blocks in blocks_of:
        for p in range(2):
            lhs = jnp.concatenate(
                [vec[2 * p, 8 * t : 8 * t + 8, :], vec[2 * p + 1, 8 * t : 8 * t + 8, :]], axis=0
            ).astype(BF16)
            raw[p, 8 * t : 8 * t + 8, :] = fold(dot_t(lhs, blocks(p)))
    even = lane % 2 == 0
    lines = []
    for p in range(2):
        y = None
        for a in range(2):
            acc = jnp.zeros((n, LANES), F32)
            for q in range(2):
                for f in range(2):
                    z = raw[p, pl.ds(4 * q + 2 * f + a, n, stride=8), :]
                    acc = jnp.where((lane // WIDTH == q) & (lane % 2 == f), z, acc)
            acc = acc + jnp.where(even, pltpu.roll(acc, LANES - 1, 1), pltpu.roll(acc, 1, 1))
            y = acc if a == 0 else jnp.where(even, y, acc)
        residual = rhs[:, LANES * p : LANES * (p + 1)] - y
        for q in range(2):
            lines.append((2 * p + q, line_rows(residual, p, q)))
    return lines


def residual_kernel(code_ref, low_ref, high_ref, rhs_ref, coupling_hbm, lower_hbm, dinv_hbm, *rest):
    res, ends_ref, ends_coupling, lower_v, dinv_v, coupling_v, sides, vec, raw, sems = rest
    n = rhs_ref.shape[0]
    cuts = [0, n // 8, n // 4, n // 2, n]
    copies = {
        lo: pltpu.make_async_copy(
            coupling_hbm.at[pl.ds(lo, hi - lo)], coupling_v.at[pl.ds(lo, hi - lo)], sems.at[i]
        )
        for i, (lo, hi) in enumerate(zip(cuts, cuts[1:]))
    }
    later = [
        pltpu.make_async_copy(lower_hbm, lower_v, sems.at[4]),
        pltpu.make_async_copy(dinv_hbm, dinv_v, sems.at[5]),
    ]
    for c in list(copies.values()) + later:
        c.start()
    where = look_up(code_ref)
    ends_ref[0:1, :] = where[0:1]
    ends_ref[1:2, :] = where[n - 1 : n]
    for side, ref in enumerate((low_ref, high_ref)):
        sides[side, 0:8, :] = jnp.zeros((8, 256), F32)
        sides[side, 8 : n + 8, :] = ref[...]
        sides[side, n + 8 : n + 16, :] = jnp.zeros((8, 256), F32)

    def rows_at(side, s, p):
        return sides[side, pl.ds(7 + s, n), LANES * p : LANES * (p + 1)]

    def blocks_of():
        for e in range(n):
            if e in copies:
                copies[e].wait()
            yield e, lambda p: coupling_v[e, LANES * p : LANES * (p + 1), :]

    for line, rows in residual_rows(n, where, rows_at, rhs_ref[...], blocks_of(), vec, raw):
        res[pl.ds(line, n, stride=8), :] = rows
        res[pl.ds(line + 4, n, stride=8), :] = rows
    ends_coupling[0] = coupling_v[0]
    ends_coupling[1] = coupling_v[n - 1]
    for c in later:
        c.wait()


def residual(code, low, high, rhs, coupling, lower, dinv):
    n = rhs.shape[0]
    return pl.pallas_call(
        residual_kernel,
        in_specs=[VMEM] * 4 + [HBM] * 3,
        out_specs=[VMEM] * 5,
        out_shape=[
            jax.ShapeDtypeStruct((8 * n, LANES), F32),
            jax.ShapeDtypeStruct((2, 512), F32),
            jax.ShapeDtypeStruct((2, 256, LANES), BF16),
            jax.ShapeDtypeStruct(lower.shape, BF16),
            jax.ShapeDtypeStruct(dinv.shape, BF16),
        ],
        scratch_shapes=[
            pltpu.VMEM((n, 256, LANES), BF16),
            pltpu.VMEM((2, n + 16, 256), F32),
            pltpu.VMEM((4, 8 * n, LANES), F32),
            pltpu.VMEM((2, 8 * n, LANES), F32),
            pltpu.SemaphoreType.DMA((6,)),
        ],
        compiler_params=pltpu.CompilerParams(vmem_limit_bytes=MOST),
        cost_estimate=pl.CostEstimate(flops=10**8, bytes_accessed=4 << 20, transcendentals=0),
        name="residual",
    )(code, low, high, rhs, coupling, lower, dinv)


def edge_terms(t, code, edge, blocks):
    row, lane = iota((8, LANES), 0), iota((8, LANES), 1)
    q, f, a = row // 4, (row // 2) % 2, row % 2
    lines = jnp.zeros((8, LANES), F32)
    for p in range(2):
        lanes = slice(LANES * p, LANES * (p + 1))
        below = jnp.broadcast_to(edge[2 * t : 2 * t + 1, lanes], (8, LANES))
        above = jnp.broadcast_to(edge[2 * t + 1 : 2 * t + 2, lanes], (8, LANES))
        w = jnp.where(f == 0, code[t : t + 1, lanes], code[t : t + 1, 256 + LANES * p : 256 + LANES * (p + 1)])
        x = jnp.where(w == 2.0 * t, below, jnp.where(w == 3.0 + 2.0 * t, above, 0.0))
        x = jnp.where(lane // WIDTH == a, jnp.where(a == q, x, swap_halves(x)), 0.0)
        y = fold(dot_t(both(x), blocks(p)))
        y = jnp.where((lane // WIDTH == q) & (lane % 2 == f), y, 0.0)
        y = y + jnp.where(lane % 2 == 0, pltpu.roll(y, LANES - 1, 1), pltpu.roll(y, 1, 1))
        y = jnp.sum(jnp.where(lane % 2 == a, y, 0.0), axis=0, keepdims=True)
        y = jnp.broadcast_to(y, (8, LANES))
        for h in range(2):
            lines = jnp.where(row % 4 == 2 * p + h, line_rows(y, p, h), lines)
    return lines


def product_and_edges_kernel(
    upper_ref, own_ref, other_ref, ends_ref, edge_ref, coupling_ref, out_ref, terms_ref
):
    out_ref[...] = multiply(upper_ref, own_ref, other_ref)
    code, edge = ends_ref[...], edge_ref[...]
    for t in range(2):
        terms_ref[t] = edge_terms(t, code, edge, lambda p: coupling_ref[t, LANES * p : LANES * (p + 1), :])


def product_and_edges(upper, own, other, ends, edge, coupling):
    return pl.pallas_call(
        product_and_edges_kernel,
        in_specs=[SMEM] + [VMEM] * 5,
        out_specs=[VMEM] * 2,
        out_shape=[
            jax.ShapeDtypeStruct((LANES, LANES), F32),
            jax.ShapeDtypeStruct((2, 8, LANES), F32),
        ],
        compiler_params=pltpu.CompilerParams(vmem_limit_bytes=4 << 20),
        name="product_and_edges",
    )(upper, own, other, ends, edge, coupling)


def chain_kernel(res, terms_ref, lower_ref, dinv_ref, sol):
    n = lower_ref.shape[0]
    blocks = n // SPAN
    ends = (0, n - 1)
    sums, own = reduce_lanes(), own_lane()
    g = [None] * blocks
    for k in range(SPAN):
        for b in range(blocks):
            e = SPAN * b + k
            balance = res[8 * e : 8 * e + 8, :]
            if e in ends:
                balance = balance - terms_ref[ends.index(e)]
            if k > 0:
                balance = balance - lying_matvec(g[b], lower_ref[e], sums, own)
            g[b] = lying_matvec(balance, dinv_ref[e], sums, own)
            sol[8 * e : 8 * e + 8, :] = g[b]


def chain(res, terms, lower, dinv):
    n = lower.shape[0]
    return pl.pallas_call(
        chain_kernel,
        in_specs=[VMEM] * 4,
        out_specs=VMEM,
        out_shape=jax.ShapeDtypeStruct((8 * n, LANES), F32),
        compiler_params=pltpu.CompilerParams(vmem_limit_bytes=MOST),
        cost_estimate=pl.CostEstimate(flops=10**9, bytes_accessed=4 << 20, transcendentals=0),
        name="chain",
    )(res, terms, lower, dinv)


def outflow_kernel(me_ref, sol, after_ref, t1_ref, t2_ref, t4_ref, g_ref, send_ref):
    me = me_ref[0]
    n = g_ref.shape[0]
    blocks = n // SPAN
    lane = iota((n, LANES), 1)
    for p in range(2):
        lanes = slice(LANES * p, LANES * (p + 1))
        g = jnp.where(
            lane < WIDTH, sol[pl.ds(2 * p, n, stride=8), :], sol[pl.ds(2 * p + 1, n, stride=8), :]
        )
        g_ref[:, lanes] = g
        w = None
        for b in range(blocks - 1, -1, -1):
            e = SPAN * b + SPAN - 1
            last = jnp.broadcast_to(g[e : e + 1], (8, LANES))
            if b < blocks - 1:
                last = times_map(last, split(expand(after_ref[b])[p]))
            w = last if w is None else w + last
        levels = [w]
        for m, t_ref in ((1, t1_ref), (2, t2_ref), (4, t4_ref)):
            moved = times_map(w, split(expand(t_ref[...])[p]))
            w = jnp.where((me // m) % 2 == 0, moved, w)
            levels.append(w)
        for half in range(2):
            target = iota((8, LANES), 0) + 8 * half
            message = jnp.zeros((8, LANES), F32)
            for lev, m in enumerate((1, 2, 4, 8)):
                reach = (target // (2 * m) == me // (2 * m)) & (target // m == me // m + 1)
                message = jnp.where(reach, levels[lev], message)
            send_ref[8 * half : 8 * half + 8, lanes] = message


def outflow(me, sol, after, t1, t2, t4):
    n = sol.shape[0] // 8
    return pl.pallas_call(
        outflow_kernel,
        in_specs=[SMEM] + [VMEM] * 5,
        out_specs=[VMEM] * 2,
        out_shape=[
            jax.ShapeDtypeStruct((n, 256), F32),
            jax.ShapeDtypeStruct((16, 256), F32),
        ],
        compiler_params=pltpu.CompilerParams(vmem_limit_bytes=4 << 20),
        name="outflow",
    )(me, sol, after, t1, t2, t4)


def finish_kernel(me_ref, got_ref, g_ref, t1_ref, t2_ref, t4_ref, spike_ref, out_ref, raw):
    n = g_ref.shape[0]
    blocks = n // SPAN
    me = me_ref[0]
    source = iota((16, LANES), 0)
    pairs = []
    for p in range(2):
        lanes = slice(LANES * p, LANES * (p + 1))
        got = got_ref[:, lanes]
        v = None
        for m, t_ref in ((8, None), (4, t4_ref), (2, t2_ref), (1, t1_ref)):
            from_here = (source // (2 * m) == me // (2 * m)) & (source // m + 1 == me // m)
            part = jnp.sum(jnp.where(from_here, got, 0.0), axis=0, keepdims=True)
            part = jnp.broadcast_to(part, (8, LANES))
            if v is None:
                v = part
            else:
                moved = times_map(v, split(expand(t_ref[...])[p]))
                v = jnp.where((me // m) % 2 == 1, moved, v) + part
        pairs.append(v)
    row, lane = iota((8, LANES), 0), iota((8, LANES), 1)

    def lines_of(pair):
        rows = [line_rows(pair[l // 2], l // 2, l % 2) for l in range(4)]
        x = rows[0]
        for l in range(1, 4):
            x = jnp.where(row % 4 == l, rows[l], x)
        return x

    sums, own = reduce_lanes(), own_lane()
    x = lines_of(pairs)
    step = 2
    for b in range(blocks):
        lhs = both(jnp.where(row // 4 == lane // WIDTH, x, 0.0))
        if b + 1 < blocks:
            e = SPAN * b + SPAN - 1
            last = [
                jnp.broadcast_to(g_ref[e : e + 1, LANES * p : LANES * (p + 1)], (8, LANES))
                for p in range(2)
            ]
            x = lying_matvec(x, spike_ref[e], sums, own) + lines_of(last)
        for k in range(0, SPAN, step):
            e = SPAN * b + k
            y = fold(dot_t(lhs, spike_ref[e : e + step].reshape(step * LANES, LANES)))
            for t in range(step):
                raw[8 * (e + t) : 8 * (e + t) + 8, :] = y[:, LANES * t : LANES * (t + 1)]
    lane_n = iota((n, LANES), 1)
    parts = []
    for a in range(2):
        acc = jnp.zeros((n, LANES), F32)
        for l in range(4):
            acc = jnp.where(lane_n % 4 == l, raw[pl.ds(4 * a + l, n, stride=8), :], acc)
        parts.append(acc)
    y = jnp.concatenate(parts, axis=1)
    src, dst = iota((256, 256), 0), iota((256, 256), 1)
    want = LANES * (dst % 2) + 4 * ((dst % WIDTH) // 2) + dst // WIDTH
    order = jnp.where(src == want, 1.0, 0.0).astype(BF16)
    high, rest = split(y)
    out_ref[...] = dot(high, order) + dot(rest, order) + g_ref[...]


def finish(me, got, g, t1, t2, t4, spike):
    n = g.shape[0]
    vmem = pl.BlockSpec(memory_space=pltpu.VMEM)
    return pl.pallas_call(
        finish_kernel,
        in_specs=[pl.BlockSpec(memory_space=pltpu.SMEM)] + [vmem] * 6,
        out_specs=vmem,
        out_shape=jax.ShapeDtypeStruct((n, 256), F32),
        scratch_shapes=[pltpu.VMEM((8 * n, LANES), F32)],
        compiler_params=pltpu.CompilerParams(vmem_limit_bytes=4 << 20),
        name="finish",
    )(me, got, g, t1, t2, t4, spike)


def flip(x, axis, bit):
    count = lax.axis_size(axis)
    return lax.ppermute(x, axis, [(i, i ^ bit) for i in range(count)])


def between(x, axis):
    count = lax.axis_size(axis)
    pairs = [(i, i + 1) for i in range(1, count - 1, 2)]
    return lax.ppermute(x, axis, pairs + [(j, i) for i, j in pairs])


def on_device(rhs, previous, dinv, lower, spike, coupling, nbr_line, nbr_shift):
    n = rhs.shape[0]
    stream, cross = lax.axis_index("stream"), lax.axis_index("cross")
    me = stream.reshape(1)

    def as_it_lies(x):
        return x.reshape(n, 4, 32, LANES).transpose(0, 2, 1, 3).reshape(n, LANES, LANES)

    far = between(previous, "cross")
    near = flip(previous, "cross", 1)
    low = jnp.where(cross % 2 == 0, far, near)
    high = jnp.where(cross % 2 == 0, near, far)
    even, odd = stream % 2 == 0, stream % 2 == 1
    first = jnp.concatenate([low[:1], high[:1]], axis=0)
    last = jnp.concatenate([low[n - 1 :], high[n - 1 :]], axis=0)
    to_mate, to_beyond = jnp.where(even, last, first), jnp.where(even, first, last)
    spike_x = as_it_lies(spike)
    own1, after = device_map(spike_x)
    t1 = flip(own1, "stream", 1)
    beyond = between(to_beyond, "stream")
    mate = flip(to_mate, "stream", 1)
    own2 = product(me % 2, own1, t1)
    mate, own2 = lax.optimization_barrier((mate, own2))
    edge = jnp.concatenate([jnp.where(odd, mate, beyond), jnp.where(odd, beyond, mate)], axis=0)
    t2 = flip(own2, "stream", 2)
    low, own2 = lax.optimization_barrier((low, own2))

    line = cross * 4 + lax.broadcasted_iota(jnp.int32, nbr_line.shape, 1)
    code = (jnp.where(nbr_line > line, 3, 0) + nbr_shift).astype(F32)
    code = code.transpose(1, 2, 0).reshape(8, n)
    coupling_x = (
        coupling.reshape(n, 4, 2, 32, LANES).transpose(0, 1, 3, 2, 4).reshape(n, 256, LANES)
    )
    res, ends, ends_coupling, lower_v, dinv_v = residual(
        code, low, high, rhs, coupling_x, as_it_lies(lower), as_it_lies(dinv)
    )
    res, own2, t2 = lax.optimization_barrier((res, own2, t2))
    own4, terms = product_and_edges((me // 2) % 2, own2, t2, ends, edge, ends_coupling)
    t4 = flip(own4, "stream", 4)
    sol = chain(res, terms, lower_v, dinv_v)
    g, send = outflow(me, sol, after, t1, t2, t4)
    got = lax.all_to_all(send, "stream", 0, 0, tiled=True)
    return finish(me, got, g, t1, t2, t4, spike_x)


def solution(mesh):
    return jax.shard_map(
        on_device,
        mesh=mesh,
        in_specs=(
            P("stream", "cross"),
            P("stream", "cross"),
            P("stream", "cross", None),
            P("stream", "cross", None),
            P("stream", "cross", None),
            P("stream", "cross", None, None),
            P("stream", "cross", None),
            P("stream", "cross", None),
        ),
        out_specs=P("stream", "cross"),
        check_vma=False,
    )
```
